32 devices in a mesh: layers: 2 (over x), row: 16 (over z, y, core).
Axes of the slice: x: 2, y: 2, z: 4, core: 2. Of those that a mesh axis runs over, the one named last changes fastest.
Arguments:
- iterate: bfloat16 [10240, 4096], P(('layers', 'row')), parts along dimension 0, may hold values from -0.0390625 to 0.0390625
Outputs:
- update: bfloat16 [10240, 4096], P(('layers', 'row')), parts along dimension 0
The draws below stay inside these ranges and needn't reach their ends.
There are 2 independent parts, one for each index of `layers`. The reference program is written for one: setup_inputs(seed, part) draws one part's arguments, and reference() takes and returns one part's arrays. A program takes and returns all parts, laid end to end along the dimension named above; each array names one. Nothing has to cross between parts.
All inputs are finite; a program needn't handle non-finite values.
Results may differ from the reference program's by a relative error of at most 0.0057.
Values may be sent and summed in bfloat16 or wider, within the bound.
A program may use at most 128 MiB of HBM per device.

```python
import math
import jax
import jax.numpy as jnp

M = 5120
D = 4096


def level_of(own_key, dims, split, least, largest):
    def one(axis_at, blocks):
        steps = jax.random.uniform(jax.random.fold_in(jax.random.fold_in(own_key, 6), axis_at), (blocks,), jnp.float32, least / len(split), largest / len(split))
        return jnp.repeat(jnp.exp(steps), dims[axis_at] // blocks).reshape((-1,) + (1,) * (len(dims) - axis_at - 1))

    loudness = one(*split[0])
    for cut in split[1:]:
        loudness = loudness * one(*cut)
    return loudness


def gaussian(stream_key, dims, scale, limit, split=(), held_as=jnp.bfloat16):
    drawn = jax.random.normal(stream_key, dims, jnp.float32) * scale
    if len(split) > 0:
        drawn = level_of(stream_key, dims, split, -0.22, 0.18) * drawn
    return jnp.clip(drawn, min=-limit, max=limit).astype(held_as)


def setup_inputs(seed: int = 0, part: int = 0) -> dict:
    keys = jax.random.split(jax.random.key(seed), 2)
    part_splits = jax.random.split(jax.random.fold_in(keys[1], part), 2)
    iterate = gaussian(part_splits[0], (M, D), (M + D + 2 * max(M, D)) ** -0.5, 0.0390625, ((0, 16),))
    return {"iterate": iterate}


def reference(iterate):
    gram = jnp.dot(iterate, iterate.T, preferred_element_type=jnp.float32).astype(jnp.bfloat16)
    carried = jnp.dot(gram, iterate, preferred_element_type=jnp.float32).astype(jnp.bfloat16)
    square = jnp.dot(carried, iterate.T, preferred_element_type=jnp.float32)
    poly = (-4.775 * gram.astype(jnp.float32) + 2.0315 * square).astype(jnp.bfloat16)
    after = 3.4445 * iterate.astype(jnp.float32) + jnp.dot(poly, iterate, preferred_element_type=jnp.float32)
    return (after * math.sqrt(max(M, D))).astype(jnp.bfloat16)
```

```python
import functools
import math

import jax
import jax.numpy as jnp
from jax import lax
from jax.experimental import pallas as pl
from jax.experimental.pallas import tpu as pltpu
from jax.sharding import PartitionSpec as P

WIDE = 512
HOP = 1
AHEAD = 3
MESH = pl.DeviceIdType.MESH
NT = (((1,), (1,)), ((), ()))
TN = (((0,), (0,)), ((), ()))


def kernel(planes, x_ref, o_ref, quad, s, part, ups, downs, acc, mid, *sems):
    (xy_s, xy_r, xc_s, xc_r, xf_s, xf_r, u_s, u_r, d_s, d_r, gy_s, gy_r, gc_s, gc_r, gf_s, gf_r) = sems
    rows, width = x_ref.shape
    chunks = width // WIDE
    steps = part.shape[0]
    layer = lax.axis_index("layers")
    me = lax.axis_index("row")
    z = me // 4
    q = me % 4
    q_core = q + 1 - 2 * (q % 2)
    q_y = (q + 2) % 4
    core = me - q + q_core
    mate = me - q + q_y
    count = 4 * planes
    above = (me + 4) % count
    below = (me + count - 4) % count

    def remote(src, dst, send, recv, to):
        return pltpu.make_async_remote_copy(
            src_ref=src, dst_ref=dst, send_sem=send, recv_sem=recv, device_id=(layer, to), device_id_type=MESH
        )

    def at(t):
        return pl.ds(pl.multiple_of(t * WIDE, WIDE), WIDE)

    def of(member):
        return pl.ds(pl.multiple_of(member * rows, 16), rows)

    def send_y(t):
        return remote(x_ref.at[:, at(t)], quad.at[of(q), at(t)], xy_s.at[t], xy_r.at[t], mate)

    def send_core(t):
        return remote(x_ref.at[:, at(t)], quad.at[of(q), at(t)], xc_s.at[t], xc_r.at[t], core)

    def pass_core(t):
        piece = quad.at[of(q_y), at(t)]
        return remote(piece, piece, xf_s.at[t], xf_r.at[t], core)

    def send_up(k):
        return remote(ups.at[k], ups.at[k], u_s.at[k], u_r.at[k], above)

    def send_down(k):
        return remote(downs.at[k], downs.at[k], d_s.at[k], d_r.at[k], below)

    def sum_y(k):
        return remote(s.at[4 * k + q], s.at[4 * k + q], gy_s.at[k], gy_r.at[k], mate)

    def sum_core(k):
        return remote(s.at[4 * k + q], s.at[4 * k + q], gc_s.at[k], gc_r.at[k], core)

    def sum_pass(k):
        return remote(s.at[4 * k + q_y], s.at[4 * k + q_y], gf_s.at[k], gf_r.at[k], core)

    def where(b):
        t = 0
        for c in range(1, chunks):
            t = t + (b + 1024 - c * (c + 1) // 2) // 1024
        return b - t * (t + 1) // 2, t

    barrier = pltpu.get_barrier_semaphore()
    for other in (core, mate, above, below):
        pl.semaphore_signal(barrier, inc=1, device_id=(layer, other), device_id_type=MESH)
    pl.semaphore_wait(barrier, 4)

    for t in range(min(AHEAD, chunks)):
        send_y(t).start()
    for t in range(chunks):
        send_core(t).start()
    quad[of(q), :] = x_ref[...]
    acc[...] = jnp.zeros_like(acc)

    def chunk(t):
        send_y(t).wait_recv()
        pass_core(t).start()
        send_y(t).wait_send()

        @pl.when(t + AHEAD < chunks)
        def _():
            send_y(t + AHEAD).start()

        send_core(t).wait_recv()
        pass_core(t).wait_recv()

    def multiply(b, into, left):
        j, t = where(b)
        into[:, at(t)] += jnp.dot(left[:, at(j)], s[b], preferred_element_type=jnp.float32)

        @pl.when(j < t)
        def _():
            into[:, at(j)] += lax.dot_general(left[:, at(t)], s[b], NT, preferred_element_type=jnp.float32)

    chunk(0)
    chunk(1)
    delay = HOP * (planes - 1)

    def step(i, carry):
        @pl.when(i + 2 < chunks)
        def _():
            chunk(i + 2)

        @pl.when(i < steps)
        def _():
            j, t = where(4 * i + q)
            part[i] = lax.dot_general(
                quad[:, at(j)], quad[:, at(t)], TN, preferred_element_type=jnp.float32
            ).astype(jnp.bfloat16)

        k = i - HOP * z

        @pl.when((k >= 0) & (k < steps))
        def _():
            @pl.when(z == 0)
            def _():
                ups[k] = part[k]

            @pl.when(z > 0)
            def _():
                send_up(k).wait_recv()
                ups[k] = (ups[k].astype(jnp.float32) + part[k].astype(jnp.float32)).astype(jnp.bfloat16)

            @pl.when(z < planes - 1)
            def _():
                send_up(k).start()

        n = i - HOP * (planes - 1 - z)

        @pl.when((n >= 0) & (n < steps))
        def _():
            @pl.when(z == planes - 1)
            def _():
                downs[n] = part[n]

            @pl.when(z < planes - 1)
            def _():
                send_down(n).wait_recv()
                downs[n] = (downs[n].astype(jnp.float32) + part[n].astype(jnp.float32)).astype(jnp.bfloat16)

            @pl.when(z > 0)
            def _():
                send_down(n).start()

        e = i - delay

        @pl.when((e >= 0) & (e < steps))
        def _():
            s[4 * e + q] = (
                ups[e].astype(jnp.float32) + downs[e].astype(jnp.float32) - part[e].astype(jnp.float32)
            ).astype(jnp.bfloat16)
            sum_y(e).start()
            sum_core(e).start()

        f = i - delay - 1

        @pl.when((f >= 0) & (f < steps))
        def _():
            sum_y(f).wait_recv()
            sum_pass(f).start()

        h = i - delay - 2

        @pl.when(h >= 0)
        def _():
            sum_core(h).wait_recv()
            sum_pass(h).wait_recv()

            def one(r, carry):
                multiply(4 * h + r, acc, x_ref)
                return carry

            lax.fori_loop(0, 4, one, 0)

        return carry

    lax.fori_loop(0, steps + delay + 2, step, 0)

    def turn(t, carry):
        first = acc[:, at(t)]
        mid[:, at(t)] = (2.0315 * first).astype(jnp.bfloat16)
        acc[:, at(t)] = 3.4445 * x_ref[:, at(t)].astype(jnp.float32) - 4.775 * first
        return carry

    lax.fori_loop(0, chunks, turn, 0)

    def last(b, carry):
        multiply(b, acc, mid)
        return carry

    lax.fori_loop(0, 4 * steps, last, 0)
    scale = math.sqrt(max(rows * count, width))

    def write(t, carry):
        o_ref[:, at(t)] = (acc[:, at(t)] * scale).astype(o_ref.dtype)
        return carry

    lax.fori_loop(0, chunks, write, 0)

    def drain_x(t, carry):
        send_core(t).wait_send()
        pass_core(t).wait_send()
        return carry

    lax.fori_loop(0, chunks, drain_x, 0)

    def drain(k, carry):
        @pl.when(z < planes - 1)
        def _():
            send_up(k).wait_send()

        @pl.when(z > 0)
        def _():
            send_down(k).wait_send()

        sum_y(k).wait_send()
        sum_core(k).wait_send()
        sum_pass(k).wait_send()
        return carry

    lax.fori_loop(0, steps, drain, 0)


def body(iterate):
    rows, width = iterate.shape
    planes = lax.axis_size("row") // 4
    chunks = width // WIDE
    blocks = chunks * (chunks + 1) // 2
    steps = blocks // 4
    block = (WIDE, WIDE)
    return pl.pallas_call(
        functools.partial(kernel, planes),
        out_shape=jax.ShapeDtypeStruct((rows, width), jnp.bfloat16),
        in_specs=[pl.BlockSpec(memory_space=pltpu.VMEM)],
        out_specs=pl.BlockSpec(memory_space=pltpu.VMEM),
        scratch_shapes=[
            pltpu.VMEM((4 * rows, width), jnp.bfloat16),
            pltpu.VMEM((blocks,) + block, jnp.bfloat16),
            pltpu.VMEM((steps,) + block, jnp.bfloat16),
            pltpu.VMEM((steps,) + block, jnp.bfloat16),
            pltpu.VMEM((steps,) + block, jnp.bfloat16),
            pltpu.VMEM((rows, width), jnp.float32),
            pltpu.VMEM((rows, width), jnp.bfloat16),
        ]
        + [pltpu.SemaphoreType.DMA((chunks,))] * 6
        + [pltpu.SemaphoreType.DMA((steps,))] * 10,
        compiler_params=pltpu.CompilerParams(
            collective_id=0, has_side_effects=True, vmem_limit_bytes=62 * 1024 * 1024
        ),
        cost_estimate=pl.CostEstimate(flops=30 * 10**9, bytes_accessed=4 * rows * width, transcendentals=0),
    )(iterate)


def solution(mesh):
    spec = P(("layers", "row"), None)
    return jax.shard_map(body, mesh=mesh, in_specs=(spec,), out_specs=spec, check_vma=False)
```

```python
import functools
import math

import jax
import jax.numpy as jnp
from jax import lax
from jax.experimental import pallas as pl
from jax.experimental.pallas import tpu as pltpu
from jax.sharding import PartitionSpec as P

WIDE = 512
SPLIT = 4
HOP = 2
LAG = 4
AHEAD = 3
MESH = pl.DeviceIdType.MESH
TN = (((0,), (0,)), ((), ()))


def kernel(planes, x_ref, o_ref, quad, s, ups, downs, acc, load, *sems):
    (xy_s, xy_r, xc_s, xc_r, xf_s, xf_r, u_s, u_r, d_s, d_r, gy_s, gy_r, gc_s, gc_r, gf_s, gf_r) = sems
    rows, width = x_ref.shape
    chunks = width // WIDE
    tall = WIDE // SPLIT
    units = ups.shape[0]
    each = 4 // SPLIT
    layer = lax.axis_index("layers")
    me = lax.axis_index("row")
    z = me // 4
    q = me % 4
    q_core = q + 1 - 2 * (q % 2)
    q_y = (q + 2) % 4
    core = me - q + q_core
    mate = me - q + q_y
    count = 4 * planes
    above = (me + 4) % count
    below = (me + count - 4) % count

    def remote(src, dst, send, recv, to):
        return pltpu.make_async_remote_copy(
            src_ref=src, dst_ref=dst, send_sem=send, recv_sem=recv, device_id=(layer, to), device_id_type=MESH
        )

    def at(t):
        return pl.ds(pl.multiple_of(t * WIDE, WIDE), WIDE)

    def of(member):
        return pl.ds(pl.multiple_of(member * rows, 16), rows)

    def send_y(t):
        piece = quad.at[of(q), at(t)]
        return remote(piece, piece, xy_s.at[t], xy_r.at[t], mate)

    def send_core(t):
        piece = quad.at[of(q), at(t)]
        return remote(piece, piece, xc_s.at[t], xc_r.at[t], core)

    def pass_core(t):
        piece = quad.at[of(q_y), at(t)]
        return remote(piece, piece, xf_s.at[t], xf_r.at[t], core)

    def send_up(k):
        return remote(ups.at[k], ups.at[k], u_s.at[k], u_r.at[k], above)

    def send_down(k):
        return remote(downs.at[k], downs.at[k], d_s.at[k], d_r.at[k], below)

    def total(u, member):
        j, t = where(4 * (u // SPLIT) + member)
        return pl.ds(pl.multiple_of(j * WIDE + (u % SPLIT) * tall, tall), tall), at(t)

    def sum_y(u):
        piece = s.at[total(u, q)]
        return remote(piece, piece, gy_s.at[u], gy_r.at[u], mate)

    def sum_core(u):
        piece = s.at[total(u, q)]
        return remote(piece, piece, gc_s.at[u], gc_r.at[u], core)

    def sum_pass(u):
        piece = s.at[total(u, q_y)]
        return remote(piece, piece, gf_s.at[u], gf_r.at[u], core)

    def where(b):
        t = 0
        for c in range(1, chunks):
            t = t + (b + 1024 - c * (c + 1) // 2) // 1024
        return b - t * (t + 1) // 2, t

    own = pltpu.make_async_copy(x_ref, quad.at[of(q)], load)
    own.start()
    barrier = pltpu.get_barrier_semaphore()
    for other in (core, mate, above, below):
        pl.semaphore_signal(barrier, inc=1, device_id=(layer, other), device_id_type=MESH)
    pl.semaphore_wait(barrier, 4)
    own.wait()

    for t in range(min(AHEAD, chunks)):
        send_y(t).start()
    for t in range(chunks):
        send_core(t).start()
    acc[...] = jnp.zeros_like(acc)

    def chunk(t):
        send_y(t).wait_recv()
        pass_core(t).start()
        send_y(t).wait_send()

        @pl.when(t + AHEAD < chunks)
        def _():
            send_y(t + AHEAD).start()

        send_core(t).wait_recv()
        pass_core(t).wait_recv()

    def multiply(b):
        j, t = where(b)
        acc[:, at(t)] += jnp.dot(quad[of(q), at(j)], s[at(j), at(t)], preferred_element_type=jnp.float32)

        @pl.when(j < t)
        def _():
            s[at(t), at(j)] = s[at(j), at(t)].T
            acc[:, at(j)] += jnp.dot(quad[of(q), at(t)], s[at(t), at(j)], preferred_element_type=jnp.float32)

    chunk(0)
    chunk(1)
    delay = HOP * (planes - 1)

    def step(i, carry):
        k = i // SPLIT

        @pl.when((i % SPLIT == 0) & (i < units))
        def _():
            @pl.when(k + 2 < chunks)
            def _():
                chunk(k + 2)

            j, t = where(4 * k + q)
            s[at(j), at(t)] = lax.dot_general(
                quad[:, at(j)], quad[:, at(t)], TN, preferred_element_type=jnp.float32
            ).astype(jnp.bfloat16)

        u = i - HOP * z

        @pl.when((u >= 0) & (u < units))
        def _():
            @pl.when(z == 0)
            def _():
                ups[u] = s[total(u, q)]

            @pl.when(z > 0)
            def _():
                send_up(u).wait_recv()
                ups[u] = (ups[u].astype(jnp.float32) + s[total(u, q)].astype(jnp.float32)).astype(jnp.bfloat16)

            @pl.when(z < planes - 1)
            def _():
                send_up(u).start()

        n = i - HOP * (planes - 1 - z)

        @pl.when((n >= 0) & (n < units))
        def _():
            @pl.when(z == planes - 1)
            def _():
                downs[n] = s[total(n, q)]

            @pl.when(z < planes - 1)
            def _():
                send_down(n).wait_recv()
                downs[n] = (downs[n].astype(jnp.float32) + s[total(n, q)].astype(jnp.float32)).astype(jnp.bfloat16)

            @pl.when(z > 0)
            def _():
                send_down(n).start()

        e = i - delay

        @pl.when((e >= 0) & (e < units))
        def _():
            mine = s[total(e, q)].astype(jnp.float32)
            s[total(e, q)] = (ups[e].astype(jnp.float32) + downs[e].astype(jnp.float32) - mine).astype(jnp.bfloat16)
            sum_y(e).start()
            sum_core(e).start()

        f = e - LAG

        @pl.when((f >= 0) & (f < units))
        def _():
            sum_y(f).wait_recv()
            sum_pass(f).start()

        h = f - 1

        @pl.when((h >= 0) & (h < units))
        def _():
            sum_core(h).wait_recv()
            sum_pass(h).wait_recv()

        @pl.when(h >= SPLIT)
        def _():
            for r in range(each):
                multiply((h - SPLIT) * each + r)

        return carry

    lax.fori_loop(0, units + delay + LAG + 1 + SPLIT, step, 0)

    def turn(t, carry):
        quad[of(q_core), at(t)] = (2.0315 * acc[:, at(t)]).astype(jnp.bfloat16)
        return carry

    lax.fori_loop(0, chunks, turn, 0)
    scale = math.sqrt(max(rows * count, width))

    def write(t, carry):
        after = jnp.dot(quad[of(q_core), :], s[:, at(t)], preferred_element_type=jnp.float32)
        after += 3.4445 * quad[of(q), at(t)].astype(jnp.float32) - 4.775 * acc[:, at(t)]
        o_ref[:, at(t)] = (after * scale).astype(o_ref.dtype)
        return carry

    lax.fori_loop(0, chunks, write, 0)

    def drain_x(t, carry):
        send_core(t).wait_send()
        pass_core(t).wait_send()
        return carry

    lax.fori_loop(0, chunks, drain_x, 0)

    def drain(k, carry):
        @pl.when(z < planes - 1)
        def _():
            send_up(k).wait_send()

        @pl.when(z > 0)
        def _():
            send_down(k).wait_send()

        sum_y(k).wait_send()
        sum_core(k).wait_send()
        sum_pass(k).wait_send()
        return carry

    lax.fori_loop(0, units, drain, 0)


def body(iterate):
    rows, width = iterate.shape
    planes = lax.axis_size("row") // 4
    chunks = width // WIDE
    blocks = chunks * (chunks + 1) // 2
    units = blocks // 4 * SPLIT
    piece = (units, WIDE // SPLIT, WIDE)
    return pl.pallas_call(
        functools.partial(kernel, planes),
        out_shape=jax.ShapeDtypeStruct((rows, width), jnp.bfloat16),
        in_specs=[pl.BlockSpec(memory_space=pl.ANY)],
        out_specs=pl.BlockSpec(memory_space=pltpu.VMEM),
        scratch_shapes=[
            pltpu.VMEM((4 * rows, width), jnp.bfloat16),
            pltpu.VMEM((width, width), jnp.bfloat16),
            pltpu.VMEM(piece, jnp.bfloat16),
            pltpu.VMEM(piece, jnp.bfloat16),
            pltpu.VMEM((rows, width), jnp.float32),
            pltpu.SemaphoreType.DMA,
        ]
        + [pltpu.SemaphoreType.DMA((chunks,))] * 6
        + [pltpu.SemaphoreType.DMA((units,))] * 10,
        compiler_params=pltpu.CompilerParams(
            collective_id=0, has_side_effects=True, vmem_limit_bytes=62 * 1024 * 1024
        ),
        cost_estimate=pl.CostEstimate(flops=30 * 10**9, bytes_accessed=4 * rows * width, transcendentals=0),
    )(iterate)


def solution(mesh):
    spec = P(("layers", "row"), None)
    return jax.shard_map(body, mesh=mesh, in_specs=(spec,), out_specs=spec, check_vma=False)
```

```python
import functools
import math

import jax
import jax.numpy as jnp
from jax import lax
from jax.experimental import pallas as pl
from jax.experimental.pallas import tpu as pltpu
from jax.sharding import PartitionSpec as P

WIDE = 512
SPLIT = 4
HOP = 2
LAG = 4
AHEAD = 3
MESH = pl.DeviceIdType.MESH
TN = (((0,), (0,)), ((), ()))


def kernel(planes, x_ref, o_ref, quad, s, ups, downs, acc, load, *sems):
    (xy_s, xy_r, xc_s, xc_r, xf_s, xf_r, u_s, u_r, d_s, d_r, gy_s, gy_r, gc_s, gc_r, gf_s, gf_r) = sems
    rows, width = x_ref.shape
    chunks = width // WIDE
    tall = WIDE // SPLIT
    units = ups.shape[0]
    each = 4 // SPLIT
    layer = lax.axis_index("layers")
    me = lax.axis_index("row")
    z = me // 4
    q = me % 4
    q_core = q + 1 - 2 * (q % 2)
    q_y = (q + 2) % 4
    core = me - q + q_core
    mate = me - q + q_y
    count = 4 * planes
    above = (me + 4) % count
    below = (me + count - 4) % count

    def remote(src, dst, send, recv, to):
        return pltpu.make_async_remote_copy(
            src_ref=src, dst_ref=dst, send_sem=send, recv_sem=recv, device_id=(layer, to), device_id_type=MESH
        )

    def at(t):
        return pl.ds(pl.multiple_of(t * WIDE, WIDE), WIDE)

    def of(member):
        return pl.ds(pl.multiple_of(member * rows, 16), rows)

    def send_y(t):
        piece = quad.at[of(q), at(t)]
        return remote(piece, piece, xy_s.at[t], xy_r.at[t], mate)

    def send_core(t):
        piece = quad.at[of(q), at(t)]
        return remote(piece, piece, xc_s.at[t], xc_r.at[t], core)

    def pass_core(t):
        piece = quad.at[of(q_y), at(t)]
        return remote(piece, piece, xf_s.at[t], xf_r.at[t], core)

    def send_up(k, skip):
        piece = ups.at[k, :, pl.ds(skip, WIDE - skip)]
        return remote(piece, piece, u_s.at[k], u_r.at[k], above)

    def send_down(k, skip):
        piece = downs.at[k, :, pl.ds(skip, WIDE - skip)]
        return remote(piece, piece, d_s.at[k], d_r.at[k], below)

    def total(u, member, skip=0):
        j, t = where(4 * (u // SPLIT) + member)
        return pl.ds(pl.multiple_of(j * WIDE + (u % SPLIT) * tall, tall), tall), pl.ds(pl.multiple_of(t * WIDE + skip, 128), WIDE - skip)

    def sum_y(u, skip):
        piece = s.at[total(u, q, skip)]
        return remote(piece, piece, gy_s.at[u], gy_r.at[u], mate)

    def sum_core(u, skip):
        piece = s.at[total(u, q, skip)]
        return remote(piece, piece, gc_s.at[u], gc_r.at[u], core)

    def sum_pass(u, skip):
        piece = s.at[total(u, q_y, skip)]
        return remote(piece, piece, gf_s.at[u], gf_r.at[u], core)

    def sum_y_in(u, skip):
        piece = s.at[total(u, q_y, skip)]
        return remote(piece, piece, gy_s.at[u], gy_r.at[u], mate)

    def sum_core_in(u, skip):
        piece = s.at[total(u, q_core, skip)]
        return remote(piece, piece, gc_s.at[u], gc_r.at[u], core)

    def sum_pass_in(u, skip):
        piece = s.at[total(u, 3 - q, skip)]
        return remote(piece, piece, gf_s.at[u], gf_r.at[u], core)

    def only(u, member, act):
        j, t = where(4 * (u // SPLIT) + member)
        part = u % SPLIT
        cut = (j == t) & (part > 0)

        @pl.when(jnp.logical_not(cut))
        def _():
            act(0)

        for p in range(1, SPLIT):

            @pl.when((j == t) & (part == p))
            def _():
                act(p * tall)

    def where(b):
        t = 0
        for c in range(1, chunks):
            t = t + (b + 1024 - c * (c + 1) // 2) // 1024
        return b - t * (t + 1) // 2, t

    own = pltpu.make_async_copy(x_ref, quad.at[of(q)], load)
    own.start()
    barrier = pltpu.get_barrier_semaphore()
    for other in (core, mate, above, below):
        pl.semaphore_signal(barrier, inc=1, device_id=(layer, other), device_id_type=MESH)
    pl.semaphore_wait(barrier, 4)
    own.wait()

    for t in range(min(AHEAD, chunks)):
        send_y(t).start()
    for t in range(chunks):
        send_core(t).start()
    acc[...] = jnp.zeros_like(acc)

    def chunk(t):
        send_y(t).wait_recv()
        pass_core(t).start()
        send_y(t).wait_send()

        @pl.when(t + AHEAD < chunks)
        def _():
            send_y(t + AHEAD).start()

        send_core(t).wait_recv()
        pass_core(t).wait_recv()

    def multiply(b):
        j, t = where(b)

        @pl.when(j == t)
        def _():
            for p in range(1, SPLIT):
                low = pl.ds(pl.multiple_of(j * WIDE + p * tall, tall), tall)
                high = pl.ds(pl.multiple_of(j * WIDE, WIDE), p * tall)
                s[low, high] = s[high, low].T

        acc[:, at(t)] += jnp.dot(quad[of(q), at(j)], s[at(j), at(t)], preferred_element_type=jnp.float32)

        @pl.when(j < t)
        def _():
            s[at(t), at(j)] = s[at(j), at(t)].T
            acc[:, at(j)] += jnp.dot(quad[of(q), at(t)], s[at(t), at(j)], preferred_element_type=jnp.float32)

    chunk(0)
    chunk(1)
    delay = HOP * (planes - 1)

    def step(i, carry):
        k = i // SPLIT

        @pl.when((i % SPLIT == 0) & (i < units))
        def _():
            @pl.when(k + 2 < chunks)
            def _():
                chunk(k + 2)

            j, t = where(4 * k + q)
            s[at(j), at(t)] = lax.dot_general(
                quad[:, at(j)], quad[:, at(t)], TN, preferred_element_type=jnp.float32
            ).astype(jnp.bfloat16)

        u = i - HOP * z

        @pl.when((u >= 0) & (u < units))
        def _():
            @pl.when(z == 0)
            def _():
                ups[u] = s[total(u, q)]

            @pl.when(z > 0)
            def _():
                only(u, q, lambda skip: send_up(u, skip).wait_recv())
                ups[u] = (ups[u].astype(jnp.float32) + s[total(u, q)].astype(jnp.float32)).astype(jnp.bfloat16)

            @pl.when(z < planes - 1)
            def _():
                only(u, q, lambda skip: send_up(u, skip).start())

        n = i - HOP * (planes - 1 - z)

        @pl.when((n >= 0) & (n < units))
        def _():
            @pl.when(z == planes - 1)
            def _():
                downs[n] = s[total(n, q)]

            @pl.when(z < planes - 1)
            def _():
                only(n, q, lambda skip: send_down(n, skip).wait_recv())
                downs[n] = (downs[n].astype(jnp.float32) + s[total(n, q)].astype(jnp.float32)).astype(jnp.bfloat16)

            @pl.when(z > 0)
            def _():
                only(n, q, lambda skip: send_down(n, skip).start())

        e = i - delay

        @pl.when((e >= 0) & (e < units))
        def _():
            mine = s[total(e, q)].astype(jnp.float32)
            s[total(e, q)] = (ups[e].astype(jnp.float32) + downs[e].astype(jnp.float32) - mine).astype(jnp.bfloat16)

            def share(skip):
                sum_y(e, skip).start()
                sum_core(e, skip).start()

            only(e, q, share)

        f = e - LAG

        @pl.when((f >= 0) & (f < units))
        def _():
            only(f, q_y, lambda skip: sum_y_in(f, skip).wait_recv())
            only(f, q_y, lambda skip: sum_pass(f, skip).start())

        h = f - 1

        @pl.when((h >= 0) & (h < units))
        def _():
            only(h, q_core, lambda skip: sum_core_in(h, skip).wait_recv())
            only(h, 3 - q, lambda skip: sum_pass_in(h, skip).wait_recv())

        @pl.when(h >= SPLIT)
        def _():
            for r in range(each):
                multiply((h - SPLIT) * each + r)

        return carry

    lax.fori_loop(0, units + delay + LAG + 1 + SPLIT, step, 0)

    def turn(t, carry):
        quad[of(q_core), at(t)] = (2.0315 * acc[:, at(t)]).astype(jnp.bfloat16)
        return carry

    lax.fori_loop(0, chunks, turn, 0)
    scale = math.sqrt(max(rows * count, width))

    def write(t, carry):
        after = jnp.dot(quad[of(q_core), :], s[:, at(t)], preferred_element_type=jnp.float32)
        after += 3.4445 * quad[of(q), at(t)].astype(jnp.float32) - 4.775 * acc[:, at(t)]
        o_ref[:, at(t)] = (after * scale).astype(o_ref.dtype)
        return carry

    lax.fori_loop(0, chunks, write, 0)

    def drain_x(t, carry):
        send_core(t).wait_send()
        pass_core(t).wait_send()
        return carry

    lax.fori_loop(0, chunks, drain_x, 0)

    def drain(k, carry):
        @pl.when(z < planes - 1)
        def _():
            only(k, q, lambda skip: send_up(k, skip).wait_send())

        @pl.when(z > 0)
        def _():
            only(k, q, lambda skip: send_down(k, skip).wait_send())

        only(k, q, lambda skip: sum_y(k, skip).wait_send())
        only(k, q, lambda skip: sum_core(k, skip).wait_send())
        only(k, q_y, lambda skip: sum_pass(k, skip).wait_send())
        return carry

    lax.fori_loop(0, units, drain, 0)


def body(iterate):
    rows, width = iterate.shape
    planes = lax.axis_size("row") // 4
    chunks = width // WIDE
    blocks = chunks * (chunks + 1) // 2
    units = blocks // 4 * SPLIT
    piece = (units, WIDE // SPLIT, WIDE)
    return pl.pallas_call(
        functools.partial(kernel, planes),
        out_shape=jax.ShapeDtypeStruct((rows, width), jnp.bfloat16),
        in_specs=[pl.BlockSpec(memory_space=pl.ANY)],
        out_specs=pl.BlockSpec(memory_space=pltpu.VMEM),
        scratch_shapes=[
            pltpu.VMEM((4 * rows, width), jnp.bfloat16),
            pltpu.VMEM((width, width), jnp.bfloat16),
            pltpu.VMEM(piece, jnp.bfloat16),
            pltpu.VMEM(piece, jnp.bfloat16),
            pltpu.VMEM((rows, width), jnp.float32),
            pltpu.SemaphoreType.DMA,
        ]
        + [pltpu.SemaphoreType.DMA((chunks,))] * 6
        + [pltpu.SemaphoreType.DMA((units,))] * 10,
        compiler_params=pltpu.CompilerParams(
            collective_id=0, has_side_effects=True, vmem_limit_bytes=62 * 1024 * 1024
        ),
        cost_estimate=pl.CostEstimate(flops=30 * 10**9, bytes_accessed=4 * rows * width, transcendentals=0),
    )(iterate)


def solution(mesh):
    spec = P(("layers", "row"), None)
    return jax.shard_map(body, mesh=mesh, in_specs=(spec,), out_specs=spec, check_vma=False)
```
